32 devices in a mesh: dp: 2 (over y), ctx: 4 (over z), wt: 4 (over x, core).
Axes of the slice: x: 2, y: 2, z: 4, core: 2. Of those that a mesh axis runs over, the one named last changes fastest.
Arguments:
- hidden: bfloat16 [8, 512, 1024], P(('dp', 'wt'), 'ctx'), may hold values from -6 to 6
- lengths: int32 [8], P(('dp', 'wt')), may hold values from 128 to 512, as said below
- buckets: int32 [1023], replicated, may hold values from 0 to 511, as said below
- w_query: bfloat16 [1024, 1024], P('wt'), may hold values from -0.1875 to 0.1875
- w_key: bfloat16 [1024, 1024], P('wt'), may hold values from -0.1875 to 0.1875
- w_value: bfloat16 [1024, 1024], P('wt'), may hold values from -0.1875 to 0.1875
- w_output: bfloat16 [1024, 1024], P('wt'), may hold values from -0.5 to 0.5
- b_query: float32 [1024], replicated, may hold values from -3 to 3
- b_key: float32 [1024], replicated, may hold values from -3 to 3
- b_value: float32 [1024], replicated, may hold values from -3 to 3
- b_output: float32 [1024], replicated, may hold values from -3 to 3
- rel_table: bfloat16 [512, 1024], P('wt'), may hold values from -6 to 6
- gain_attn: float32 [1024], replicated, may hold values from 0.5 to 1.5
- shift_attn: float32 [1024], replicated, may hold values from -1.2 to 1.2
- w_inner: bfloat16 [1024, 4096], P('wt'), may hold values from -0.1875 to 0.1875
- b_inner: float32 [4096], replicated, may hold values from -3 to 3
- w_outer: bfloat16 [4096, 1024], P('wt'), may hold values from -0.125 to 0.125
- b_outer: float32 [1024], replicated, may hold values from -3 to 3
- gain_ffn: float32 [1024], replicated, may hold values from 0.5 to 1.5
- shift_ffn: float32 [1024], replicated, may hold values from -1.2 to 1.2
- cotangent: bfloat16 [8, 512, 1024], P(('dp', 'wt'), 'ctx'), may hold values from -6 to 6
Outputs:
- output: bfloat16 [8, 512, 1024], P(('dp', 'wt'), 'ctx')
- grad_hidden: bfloat16 [8, 512, 1024], P(('dp', 'wt'), 'ctx')
- grad_w_query: float32 [1024, 1024], P('wt')
- grad_w_key: float32 [1024, 1024], P('wt')
- grad_w_value: float32 [1024, 1024], P('wt')
- grad_w_output: float32 [1024, 1024], P('wt')
- grad_b_query: float32 [1024], P('wt')
- grad_b_key: float32 [1024], P('wt')
- grad_b_value: float32 [1024], P('wt')
- grad_b_output: float32 [1024], P('wt')
- grad_rel_table: float32 [512, 1024], P('wt')
- grad_gain_attn: float32 [1024], P('wt')
- grad_shift_attn: float32 [1024], P('wt')
- grad_w_inner: float32 [1024, 4096], P('wt')
- grad_b_inner: float32 [4096], P('wt')
- grad_w_outer: float32 [4096, 1024], P('wt')
- grad_b_outer: float32 [1024], P('wt')
- grad_gain_ffn: float32 [1024], P('wt')
- grad_shift_ffn: float32 [1024], P('wt')
The draws below stay inside these ranges and needn't reach their ends.
Inputs may be any that keep to these rules, and one draw needn't show every extreme that they name: lengths[n] is the number of valid leading slots of sequence n; one sequence has exactly 512 and another exactly 128. buckets[r + 511] is the bucket of relative distance r = i - j; it never falls as r rises, equals 256 + r for |r| <= 128, and is 0 at r = 1 - 512 and 511 at r = 511.
All inputs are finite; a program needn't handle non-finite values.
Results may differ from the reference program's by a relative error of at most 0.03.
Values may be sent and summed in bfloat16 or wider, within the bound.
A program may use at most 320 MiB of HBM per device.

```python
import math
import jax
import jax.numpy as jnp
from jax import lax

D = 1024
HEADS = 16
FF = 4096
SPAN = 256
HEAD_DIM = 64
BUCKETS = 512
SLOTS = 512
SEQS = 8


def draw_lengths(key, part):
    key = jax.random.fold_in(key, 11)
    draw_first, draw_second, draw_third = jax.random.split(key, 3)
    values_out = jax.random.randint(draw_first, (SEQS,), SLOTS // 4, SLOTS + 1)
    longest = jax.random.randint(draw_second, (), 0, SEQS)
    shortest = (longest + 1 + jax.random.randint(draw_third, (), 0, SEQS - 1)) % SEQS
    values_out = values_out.at[longest].set(SLOTS).at[shortest].set(SLOTS // 4)
    return values_out.astype(jnp.int32)


def bucket_side(step_bits, level_cap):
    reach = jnp.arange(SLOTS, dtype=jnp.int32)
    half_span = SPAN // 2
    growth = jnp.cumsum(jnp.where(reach > half_span, step_bits, 0)).astype(jnp.int32)
    level = jnp.minimum(jnp.minimum(reach, half_span) + growth, level_cap)
    return jnp.where(reach == SLOTS - 1, level_cap, level).astype(jnp.int32)


def draw_buckets(key, part):
    key = jax.random.fold_in(key, 23)
    upper_key, lower_key = jax.random.split(key)
    upper_bits = jax.random.randint(upper_key, (SLOTS,), 0, 2)
    lower_bits = jax.random.randint(lower_key, (SLOTS,), 0, 2)
    upper = SPAN + bucket_side(upper_bits, SPAN - 1)
    lower = SPAN - bucket_side(lower_bits, SPAN)
    return jnp.concatenate([lower[1:][::-1], upper]).astype(jnp.int32)


def level_of(own_key, dims, pieces, smallest, largest):
    factor_of = 1.0
    for axis_at, blocks in pieces:
        draws = jax.random.uniform(jax.random.fold_in(jax.random.fold_in(own_key, 6), axis_at), (blocks,), jnp.float32, smallest / len(pieces), largest / len(pieces))
        factor_of = factor_of * jnp.repeat(jnp.exp(draws), dims[axis_at] // blocks).reshape((-1,) + (1,) * (len(dims) - 1 - axis_at))
    return factor_of


def noise(rng, dims, deviation, bound, shards=(), kind=jnp.bfloat16):
    array = deviation * jax.random.normal(rng, dims, jnp.float32)
    if shards:
        array = array * level_of(rng, dims, shards, -0.22, 0.18)
    return jnp.clip(array, -bound, bound).astype(kind)


def setup_inputs(seed: int = 0) -> dict:
    key_of = jax.random.split(jax.random.key(seed), 22)
    hidden = noise(key_of[0], (SEQS, SLOTS, D), 1.0, 6.0, ((0, 8), (1, 4)))
    lengths = draw_lengths(jax.random.fold_in(key_of[21], 71), 0)
    buckets = draw_buckets(jax.random.fold_in(key_of[21], 71), 0)
    w_query = noise(key_of[3], (D, D), D ** -0.5, 0.1875, ((0, 4),))
    w_key = noise(key_of[4], (D, D), D ** -0.5, 0.1875, ((0, 4),))
    w_value = noise(key_of[5], (D, D), D ** -0.5, 0.1875, ((0, 4),))
    w_output = noise(key_of[6], (D, D), (D // 8) ** -0.5, 0.5, ((0, 4),))
    b_query = noise(key_of[7], (D,), 0.5, 3.0, (), jnp.float32)
    b_key = noise(key_of[8], (D,), 0.5, 3.0, (), jnp.float32)
    b_value = noise(key_of[9], (D,), 0.5, 3.0, (), jnp.float32)
    b_output = noise(key_of[10], (D,), 0.5, 3.0, (), jnp.float32)
    rel_table = noise(key_of[11], (BUCKETS, D), 1.0, 6.0, ((0, 4),))
    gain_attn = jnp.clip(1.0 + 0.1 * jax.random.normal(key_of[12], (D,), jnp.float32), 0.5, 1.5)
    shift_attn = noise(key_of[13], (D,), 0.2, 1.2, (), jnp.float32)
    w_inner = noise(key_of[14], (D, FF), D ** -0.5, 0.1875, ((0, 4),))
    b_inner = noise(key_of[15], (FF,), 0.5, 3.0, (), jnp.float32)
    w_outer = noise(key_of[16], (FF, D), (FF // 2) ** -0.5, 0.125, ((0, 4),))
    b_outer = noise(key_of[17], (D,), 0.5, 3.0, (), jnp.float32)
    gain_ffn = jnp.clip(1.0 + 0.1 * jax.random.normal(key_of[18], (D,), jnp.float32), 0.5, 1.5)
    shift_ffn = noise(key_of[19], (D,), 0.2, 1.2, (), jnp.float32)
    cotangent = noise(key_of[20], (SEQS, SLOTS, D), 1.0, 6.0, ((0, 8), (1, 4)))
    return dict(hidden=hidden, lengths=lengths, buckets=buckets, w_query=w_query, w_key=w_key, w_value=w_value, w_output=w_output, b_query=b_query, b_key=b_key, b_value=b_value, b_output=b_output, rel_table=rel_table, gain_attn=gain_attn, shift_attn=shift_attn, w_inner=w_inner, b_inner=b_inner, w_outer=w_outer, b_outer=b_outer, gain_ffn=gain_ffn, shift_ffn=shift_ffn, cotangent=cotangent)


EPSILON = 1e-07

@jax.custom_vjp
def low(v):
    return lax.optimization_barrier(v.astype(jnp.bfloat16)).astype(jnp.float32)

@jax.custom_vjp
def low_back(v):
    return v

def low_keep(v):
    return (low(v), None)

def low_pass(kept, grad):
    return (grad,)

def back_keep(v):
    return (v, None)

def back_low(kept, grad):
    return (low(grad),)
low.defvjp(low_keep, low_pass)
low_back.defvjp(back_keep, back_low)

def both_ways(values_in):
    return low_back(low(values_in))

def matmul(left_side, right_side):
    return jnp.dot(left_side, right_side, precision=lax.Precision.HIGHEST)

def normalize(values_in, gain_row, shift_row):
    row_mean = lax.optimization_barrier(jnp.mean(values_in, axis=-1, keepdims=True))
    centred = values_in - row_mean
    row_var = lax.optimization_barrier(jnp.mean(centred * centred, axis=-1, keepdims=True))
    return centred * lax.rsqrt(row_var + EPSILON) * gain_row + shift_row

def pick_bucket(score_table, bucket_index):
    return jnp.take_along_axis(score_table, bucket_index[None], axis=2)

def forward(hidden, lengths, buckets, w_query, w_key, w_value, w_output, b_query, b_key, b_value, b_output, rel_table, gain_attn, shift_attn, w_inner, b_inner, w_outer, b_outer, gain_ffn, shift_ffn):
    slot_count = hidden.shape[1]
    model_width = hidden.shape[2]
    score_scale = 1.0 / math.sqrt(3 * HEAD_DIM)
    rel_key = both_ways(matmul(rel_table, w_key) + b_key).reshape(-1, HEADS, HEAD_DIM)
    rel_query = both_ways(matmul(rel_table, w_query) + b_query).reshape(-1, HEADS, HEAD_DIM)
    positions = jnp.arange(slot_count, dtype=jnp.int32)
    near_index = buckets[positions[:, None] - positions[None, :] + slot_count - 1]

    def one_sequence(tokens, seq_length):
        key_valid = positions < seq_length
        query_h = both_ways(matmul(tokens, w_query) + b_query).reshape(slot_count, HEADS, HEAD_DIM)
        key_h = both_ways(matmul(tokens, w_key) + b_key).reshape(slot_count, HEADS, HEAD_DIM)
        value_h = both_ways(matmul(tokens, w_value) + b_value).reshape(slot_count, HEADS, HEAD_DIM)
        content = jnp.einsum('qhd,khd->hqk', query_h, key_h, precision=lax.Precision.HIGHEST)
        along = low_back(jnp.einsum('qhd,rhd->hqr', query_h, rel_key, precision=lax.Precision.HIGHEST))
        across = low_back(jnp.einsum('khd,rhd->hkr', key_h, rel_query, precision=lax.Precision.HIGHEST))
        raw = content + pick_bucket(along, near_index) + jnp.transpose(pick_bucket(across, near_index), (0, 2, 1))
        scores = jnp.where(key_valid[None, None, :], low_back(raw) * score_scale, -1000000000.0)
        row_top = lax.optimization_barrier(jnp.max(scores, axis=2, keepdims=True))
        exponent = jnp.exp(scores - row_top)
        probs_full = exponent / lax.optimization_barrier(jnp.sum(exponent, axis=2, keepdims=True))
        context = jnp.einsum('hqk,khd->qhd', low(probs_full), value_h, precision=lax.Precision.HIGHEST)
        context = both_ways(context.reshape(slot_count, model_width))
        residual_one = tokens + low_back(matmul(context, w_output) + b_output)
        normed_one = normalize(residual_one, gain_attn, shift_attn)
        inner_pre = low_back(matmul(low(normed_one), w_inner) + b_inner)
        active = low(jax.nn.gelu(inner_pre, approximate=False))
        residual_two = normed_one + low_back(matmul(active, w_outer) + b_outer)
        return normalize(residual_two, gain_ffn, shift_ffn)
    checked_step = jax.checkpoint(one_sequence)

    def run_one(seq_pair):
        return checked_step(seq_pair[0], seq_pair[1])
    return lax.map(run_one, (hidden, lengths))

def widen(values_in):
    return values_in.astype(jnp.float32)

def reference(hidden, lengths, buckets, w_query, w_key, w_value, w_output, b_query, b_key, b_value, b_output, rel_table, gain_attn, shift_attn, w_inner, b_inner, w_outer, b_outer, gain_ffn, shift_ffn, cotangent):

    def apply_layer(tokens, p_query, p_key, p_value, p_output, c_query, c_key, c_value, c_output, p_rel, g_attn, s_attn, p_inner, c_inner, p_outer, c_outer, g_ffn, s_ffn):
        return forward(tokens, lengths, buckets, p_query, p_key, p_value, p_output, c_query, c_key, c_value, c_output, p_rel, g_attn, s_attn, p_inner, c_inner, p_outer, c_outer, g_ffn, s_ffn)
    result, pullback = jax.vjp(apply_layer, widen(hidden), widen(w_query), widen(w_key), widen(w_value), widen(w_output), b_query, b_key, b_value, b_output, widen(rel_table), gain_attn, shift_attn, widen(w_inner), b_inner, widen(w_outer), b_outer, gain_ffn, shift_ffn)
    slot_count = hidden.shape[1]
    slot_valid = (jnp.arange(slot_count, dtype=jnp.int32)[None, :] < lengths[:, None]).astype(jnp.float32)
    grads = pullback(widen(cotangent) * slot_valid[:, :, None])
    return (result.astype(jnp.bfloat16), grads[0].astype(jnp.bfloat16), grads[1], grads[2], grads[3], grads[4], grads[5], grads[6], grads[7], grads[8], grads[9], grads[10], grads[11], grads[12], grads[13], grads[14], grads[15], grads[16], grads[17])
```

```python
import functools
import math

import jax
import jax.numpy as jnp
from jax import lax
from jax.experimental import pallas as pl
from jax.experimental.pallas import tpu as pltpu
from jax.sharding import PartitionSpec as P_

BF=jnp.bfloat16; F32=jnp.float32
def dot(a,b): return jnp.dot(a,b,preferred_element_type=F32)
def dot_t(a,b): return lax.dot_general(a,b,(((1,),(1,)),((),())),preferred_element_type=F32)
def tdot(a,b): return lax.dot_general(a,b,(((0,),(0,)),((),())),preferred_element_type=F32)
BLK=128
HD=64

def lane_mask(half):
    lane=lax.broadcasted_iota(jnp.int32,(1,2*HD),1)
    return ((lane<HD) if half==0 else (lane>=HD))
def only(x,half):
    return jnp.where(lane_mask(half),x,jnp.zeros((),x.dtype))

def attn_fwd(q,k,v,rkf,rqf,P,across,ctx,length,slots,cols,scale):
    nb=slots//BLK
    win=slots+BLK
    for p in range(cols//(2*HD)):
        L=slice(p*2*HD,(p+1)*2*HD)
        for half in range(2):
            h=2*p+half
            def kb_body(J,c):
                r0=pl.multiple_of(J*BLK,BLK)
                w0=pl.multiple_of((nb-1-J)*BLK,BLK)
                kb=only(k[pl.ds(r0,BLK),L],half)
                b=dot_t(kb,rqf[pl.ds(w0,win),L])
                b=pltpu.roll(b,win-(BLK-1),1,stride=1,stride_axis=0)[:,:slots]
                across[:,pl.ds(r0,BLK)]=b.T
                return c
            lax.fori_loop(0,nb,kb_body,0,unroll=True)
            def qb_body(I,c):
                r0=pl.multiple_of(I*BLK,BLK)
                w0=pl.multiple_of((nb-1-I)*BLK,BLK)
                qb=only(q[pl.ds(r0,BLK),L],half)
                al=dot_t(qb,rkf[pl.ds(w0,win),L])
                al=pltpu.roll(al,win-(BLK-1),1,stride=1,stride_axis=0)[:,:slots]
                raw=dot_t(qb,k[:,L])+al+across[pl.ds(r0,BLK),:]
                valid=lax.broadcasted_iota(jnp.int32,(1,slots),1)<length
                sc=jnp.where(valid,raw*scale,-1e9)
                top=jnp.max(sc,axis=1,keepdims=True)
                e=jnp.exp(sc-top)
                pr=e/jnp.sum(e,axis=1,keepdims=True)
                P[h,pl.ds(r0,BLK),:]=pr
                c2=dot(pr.astype(BF),v[:,L])
                if half==0: ctx[pl.ds(r0,BLK),L]=c2.astype(BF)
                else: ctx[pl.ds(r0,BLK),L]=jnp.where(lane_mask(1),c2.astype(BF),ctx[pl.ds(r0,BLK),L])
                return c
            lax.fori_loop(0,nb,qb_body,0,unroll=True)

def attn_bwd(q,k,v,dctx,rks,rqs,P,ds,dq,dk,dv,grk,grq,slots,cols,scale):
    nb=slots//BLK
    win=slots+BLK
    RW=256
    ii=lax.broadcasted_iota(jnp.int32,(RW,RW),0); jj=lax.broadcasted_iota(jnp.int32,(RW,RW),1)
    flip=jnp.where(ii+jj==RW-1,1.0,0.0).astype(BF)
    def unskew(x):
        parts=[dot(x[:,c*RW:(c+1)*RW],flip) for c in range(slots//RW)][::-1]
        y=jnp.concatenate(parts+[jnp.zeros((BLK,BLK),F32)],axis=1)
        return pltpu.roll(y,0,1,stride=1,stride_axis=0).astype(BF)
    grk[...]=jnp.zeros_like(grk); grq[...]=jnp.zeros_like(grq)
    for p in range(cols//(2*HD)):
        L=slice(p*2*HD,(p+1)*2*HD)
        dq2=None
        for half in range(2):
            h=2*p+half
            kh=only(k[:,L],half);
            def qb_body(I,c):
                r0=pl.multiple_of(I*BLK,BLK)
                rows=pl.ds(r0,BLK)
                qb=only(q[rows,L],half)
                db=only(dctx[rows,L],half)
                dp=dot_t(db,v[:,L])
                pr=P[h,rows,:]
                ri=jnp.sum(pr*dp,axis=1,keepdims=True)
                d=(pr*(dp-ri)*scale).astype(BF)
                ds[rows,:]=d
                u=unskew(d)
                w=pl.ds(r0,win)
                g=dot(d,kh)+dot(u,only(rks[w,L],half))
                if half==0: dq[rows,L]=g
                else: dq[rows,L]+=g
                grk[w,L]+=tdot(u,qb)
                return c
            lax.fori_loop(0,nb,qb_body,0,unroll=True)
            qh=only(q[:,L],half); dh=only(dctx[:,L],half)
            def kb_body(J,c):
                r0=pl.multiple_of(J*BLK,BLK)
                rows=pl.ds(r0,BLK)
                kb=only(k[rows,L],half)
                dt=ds[:,rows].T
                u=unskew(dt)
                w=pl.ds(r0,win)
                g=dot(dt,qh)+dot(u,only(rqs[w,L],half))
                gv=tdot(P[h,:,rows].astype(BF),dh)
                if half==0: dk[rows,L]=g; dv[rows,L]=gv
                else: dk[rows,L]+=g; dv[rows,L]+=gv
                grq[w,L]+=tdot(u,kb)
                return c
            lax.fori_loop(0,nb,kb_body,0,unroll=True)


EPS = 1e-07
HEADS = 16

def col_sum(x):
    return jnp.sum(x.astype(F32), axis=0)

def normalize(values_in, gain_row, shift_row):
    row_mean = jnp.mean(values_in, axis=-1, keepdims=True)
    centred = values_in - row_mean
    row_var = jnp.mean(centred * centred, axis=-1, keepdims=True)
    return centred * lax.rsqrt(row_var + EPS) * gain_row + shift_row

V = pl.BlockSpec(memory_space=pltpu.VMEM)
S = pl.BlockSpec(memory_space=pltpu.SMEM)
PARAMS = pltpu.CompilerParams(vmem_limit_bytes=48 * 2**20)

def fwd_kernel(scale, len_ref, q, k, v, rkf, rqf, ctx, P, across):
    slots, cols = q.shape
    attn_fwd(q, k, v, rkf, rqf, P, across, ctx, len_ref[0], slots, cols, scale)

def bwd_kernel(scale, q, k, v, dctx, rks, rqs, P, dq, dk, dv, grk, grq, ds):
    slots, cols = q.shape
    attn_bwd(q, k, v, dctx, rks, rqs, P, ds, dq, dk, dv, grk, grq, slots, cols, scale)

def per_device(hidden, lengths, buckets, w_query, w_key, w_value, w_output, b_query, b_key, b_value, b_output,
               rel_table, gain_attn, shift_attn, w_inner, b_inner, w_outer, b_outer, gain_ffn, shift_ffn, cotangent):
    nw = lax.axis_size("wt"); nc = lax.axis_size("ctx"); nd = lax.axis_size("dp")
    group = ("dp", "ctx"); ng = nd * nc
    tokens = hidden[0]
    rows, D = tokens.shape
    slots = rows * nc
    cols = D // nw
    wi = lax.axis_index("wt"); ci = lax.axis_index("ctx")
    scale = 1.0 / math.sqrt(3 * HD)
    a2a = lambda x, ax, s, c: lax.all_to_all(x, ax, split_axis=s, concat_axis=c, tiled=True)
    ag = lambda x: lax.all_gather(x, "wt", axis=0, tiled=True)
    rs = lambda x: lax.psum_scatter(x.astype(BF), "wt", scatter_dimension=0, tiled=True).astype(F32)
    tok_all = ag(tokens)
    rel_all = ag(rel_table)
    wqkv = jnp.concatenate([w_query.reshape(cols, nw, cols), w_key.reshape(cols, nw, cols), w_value.reshape(cols, nw, cols)], axis=2)
    wqkv = a2a(wqkv.reshape(cols, nw * 3 * cols), "wt", 1, 0)
    win_c = a2a(w_inner, "wt", 1, 0)
    cut = lambda b, n: lax.dynamic_slice_in_dim(b, wi * n, n)
    bq, bk, bv = cut(b_query, cols), cut(b_key, cols), cut(b_value, cols)
    wq_c, wk_c, wv_c = wqkv[:, :cols], wqkv[:, cols:2*cols], wqkv[:, 2*cols:]
    qkv = (dot(tok_all, wqkv) + jnp.concatenate([bq, bk, bv])).astype(BF)
    qkv = a2a(qkv, "ctx", 0, 0)
    q, k, v = qkv[:, :cols], qkv[:, cols:2*cols], qkv[:, 2*cols:]
    rk = (dot(rel_all, wk_c) + bk).astype(BF)
    rq = (dot(rel_all, wq_c) + bq).astype(BF)
    nb = rk.shape[0]
    pad = jnp.full((2 * slots - buckets.shape[0],), -1, jnp.int32)
    bs = jnp.concatenate([buckets, pad]); bf_ = jnp.concatenate([buckets[::-1], pad])
    ids = jnp.arange(nb, dtype=jnp.int32)
    hot_s = (bs[:, None] == ids[None, :]).astype(BF); hot_f = (bf_[:, None] == ids[None, :]).astype(BF)
    rr = jnp.concatenate([rk, rq], axis=1)
    rf = dot(hot_f, rr).astype(BF); rsn = dot(hot_s, rr).astype(BF)
    length = lax.dynamic_slice_in_dim(lax.all_gather(lengths, "wt", axis=0, tiled=True), ci, 1)
    ctx, P = pl.pallas_call(functools.partial(fwd_kernel, scale), name="attn_forward",
        out_shape=[jax.ShapeDtypeStruct((slots, cols), BF), jax.ShapeDtypeStruct((cols // HD, slots, slots), F32)],
        in_specs=[S] + [V] * 5, out_specs=[V, V], scratch_shapes=[pltpu.VMEM((slots, slots), F32)], compiler_params=PARAMS,
    )(length, q, k, v, rf[:, :cols], rf[:, cols:])
    ctx4 = a2a(ctx, "ctx", 0, 0)
    res_one = tokens.astype(F32) + rs(dot(ctx4, w_output)) + b_output
    normed = normalize(res_one, gain_attn, shift_attn)
    nl_all = ag(normed.astype(BF))
    inner_pre = dot(nl_all, win_c) + cut(b_inner, win_c.shape[1])
    active = jax.nn.gelu(inner_pre, approximate=False).astype(BF)
    res_two = normed + rs(dot(active, w_outer)) + b_outer
    result = normalize(res_two, gain_ffn, shift_ffn)
    pos = ci * rows + jnp.arange(rows, dtype=jnp.int32)
    seed = cotangent[0].astype(F32) * (pos < lengths[0]).astype(F32)[:, None]
    d_res_two, g_gain_ffn, g_shift_ffn = jax.vjp(normalize, res_two, gain_ffn, shift_ffn)[1](seed)
    db_all = ag(d_res_two.astype(BF))
    d_active = dot_t(db_all, w_outer)
    d_inner = jax.vjp(functools.partial(jax.nn.gelu, approximate=False), inner_pre)[1](d_active)[0].astype(BF)
    g_outer = tdot(active, db_all)
    g_inner = tdot(nl_all, d_inner)
    d_normed = d_res_two + rs(dot_t(d_inner, win_c))
    d_res_one, g_gain_attn, g_shift_attn = jax.vjp(normalize, res_one, gain_attn, shift_attn)[1](d_normed)
    da_all = ag(d_res_one.astype(BF))
    g_output = tdot(ctx4, da_all)
    dctx = a2a(dot_t(da_all, w_output).astype(BF), "ctx", 0, 0)
    dq, dk, dv, grk, grq = pl.pallas_call(functools.partial(bwd_kernel, scale), name="attn_backward",
        out_shape=[jax.ShapeDtypeStruct((slots, cols), F32)] * 3 + [jax.ShapeDtypeStruct((2 * slots, cols), F32)] * 2,
        in_specs=[V] * 7, out_specs=[V] * 5, scratch_shapes=[pltpu.VMEM((slots, slots), BF)], compiler_params=PARAMS,
    )(q, k, v, dctx, rsn[:, :cols], rsn[:, cols:], P)
    d4 = a2a(jnp.concatenate([dq, dk, dv], axis=1).astype(BF), "ctx", 0, 0)
    grr = tdot(hot_s, jnp.concatenate([grk, grq], axis=1).astype(BF)).astype(BF)
    grk_b, grq_b = grr[:, :cols], grr[:, cols:]
    g_qkv = tdot(tok_all, d4) + tdot(rel_all, jnp.concatenate([grq_b, grk_b, jnp.zeros_like(grk_b)], axis=1))
    g_rel = rs(dot_t(grk_b, wk_c) + dot_t(grq_b, wq_c))
    grad_tokens = d_res_one + rs(dot_t(d4, wqkv))
    by_rows = jnp.concatenate([g_outer, g_output, g_rel], axis=0).astype(BF)
    def by_group(g):
        n = g.shape[0] // (nw * ng)
        return g.astype(BF).reshape(nw, ng, n, g.shape[1]).transpose(1, 0, 2, 3).reshape(ng * nw * n, g.shape[1])
    by_cols = jnp.concatenate([by_group(g_inner), by_group(g_qkv)], axis=1)
    scat = lambda x: lax.psum_scatter(x, group, scatter_dimension=0, tiled=True)
    gat = lambda x: lax.all_gather(x, group, axis=0, tiled=True)
    row_part = gat(scat(by_rows)).astype(F32)
    mine = scat(by_cols)
    mine = a2a(mine, "wt", 0, 1)
    col_part = gat(mine).astype(F32)
    n_in = g_inner.shape[1]
    width = n_in + 3 * cols
    col_part = col_part.reshape(cols, nw, width)
    gi = col_part[:, :, :n_in].reshape(cols, nw * n_in)
    pick = lambda i: col_part[:, :, n_in + i * cols: n_in + (i + 1) * cols].reshape(cols, nw * cols)
    small_sh = jnp.concatenate([col_sum(d4) + jnp.concatenate([col_sum(grq_b), col_sum(grk_b), jnp.zeros((cols,), F32)]), col_sum(d_inner)])
    small_sh = lax.psum(small_sh, group)
    small = lax.psum(jnp.concatenate([col_sum(d_res_one.astype(BF)), col_sum(d_res_two.astype(BF)), g_gain_attn, g_shift_attn, g_gain_ffn, g_shift_ffn]), ("dp", "ctx", "wt"))
    sm = lambda i: cut(small[i * D:(i + 1) * D], cols)
    nf = g_outer.shape[0]
    return (result.astype(BF)[None], grad_tokens.astype(BF)[None], pick(0), pick(1), pick(2), row_part[nf:nf + cols],
        small_sh[:cols], small_sh[cols:2 * cols], small_sh[2 * cols:3 * cols], sm(0), row_part[nf + cols:], sm(2), sm(3),
        gi, small_sh[3 * cols:], row_part[:nf], sm(1), sm(4), sm(5))

def solution(mesh):
    in_specs = (
        P_(("dp", "wt"), "ctx", None),
        P_(("dp", "wt")),
        P_(),
        P_("wt", None),
        P_("wt", None),
        P_("wt", None),
        P_("wt", None),
        P_(),
        P_(),
        P_(),
        P_(),
        P_("wt", None),
        P_(),
        P_(),
        P_("wt", None),
        P_(),
        P_("wt", None),
        P_(),
        P_(),
        P_(),
        P_(("dp", "wt"), "ctx", None),
    )
    out_specs = (
        P_(("dp", "wt"), "ctx", None),
        P_(("dp", "wt"), "ctx", None),
        P_("wt", None),
        P_("wt", None),
        P_("wt", None),
        P_("wt", None),
        P_("wt"),
        P_("wt"),
        P_("wt"),
        P_("wt"),
        P_("wt", None),
        P_("wt"),
        P_("wt"),
        P_("wt", None),
        P_("wt"),
        P_("wt", None),
        P_("wt"),
        P_("wt"),
        P_("wt"),
    )
    return jax.shard_map(
        per_device, mesh=mesh, in_specs=in_specs, out_specs=out_specs, check_vma=False
    )
```
